32 devices in a mesh: blk: 8 (over y, x, core), head: 4 (over z).
Axes of the slice: x: 2, y: 2, z: 4, core: 2. Of those that a mesh axis runs over, the one named last changes fastest.
Arguments:
- tokens: bfloat16 [512, 4096], P('blk', 'head'), may hold values from -6 to 6
- queries: bfloat16 [512, 36864], P('blk', 'head'), may hold values from -600 to 600
- latents: bfloat16 [512, 576], P('blk'), may hold values from -6 to 6
- value_up: bfloat16 [64, 512, 128], P('head'), may hold values from -0.25 to 0.25
- out_proj: bfloat16 [8192, 4096], P('head', 'blk'), may hold values from -0.09375 to 0.09375
- expert_ids: int32 [512, 8], P('blk'), may hold values from 0 to 31, all different within a row; in each aligned block of 64 rows (0 to 63, 64 to 127, ...) at most 20 rows name the same one
- expert_gates: float32 [512, 8], P('blk'), may hold values from 0.05 to 0.5
- w_gate: bfloat16 [32, 4096, 2048], P('blk', None, 'head'), may hold values from -0.09375 to 0.09375
- w_up: bfloat16 [32, 4096, 2048], P('blk', None, 'head'), may hold values from -0.09375 to 0.09375
- w_down: bfloat16 [32, 2048, 4096], P('blk', None, 'head'), may hold values from -0.125 to 0.125
Outputs:
- result: bfloat16 [512, 4096], P('blk', 'head')
The draws below stay inside these ranges and needn't reach their ends.
Inputs may be any that keep to these rules, and one draw needn't show every extreme that they name: `expert_ids`: among the tokens of one index of blk (aligned blocks of 64 rows) at most 20 choose one expert, and some expert is chosen by exactly 20 of them; the experts of one row differ.
All inputs are finite; a program needn't handle non-finite values.
Results may differ from the reference program's by a relative error of at most 0.013.
Values may be sent and summed in bfloat16 or wider, within the bound.
A program may use at most 128 MiB of HBM per device.

```python
import math
import jax
import jax.numpy as jnp
import numpy as np
from jax import lax

D = 4096
LAT = 512
ROPE = 64
QKNOPE = 128
VDIM = 128
HEADS = 64
FF = 2048
EXPERTS = 32
TOPK = 8
TOK_DEV = 64
CAP = 20
TOKENS = 512
N_BLK = 8


def latent_table(key):
    base = jax.random.truncated_normal(jax.random.fold_in(key, 11), -6.0, 6.0, (TOKENS, LAT + ROPE), jnp.float32)
    return base


def draw_latents(key, part):
    return latent_table(key).astype(jnp.bfloat16)


def draw_queries(key, part):
    base = jax.random.truncated_normal(jax.random.fold_in(key, 23), -6.0, 6.0, (TOKENS, HEADS, LAT + ROPE), jnp.float32)
    return base.reshape(TOKENS, HEADS * (LAT + ROPE)).astype(jnp.bfloat16)


def levels(own_key, dims, cuts, low, top_value):
    gain = 1.0
    for dim, shards_of in cuts:
        steps = jax.random.uniform(jax.random.fold_in(jax.random.fold_in(own_key, 6), dim), (shards_of,), jnp.float32, low / len(cuts), top_value / len(cuts))
        gain = gain * jnp.repeat(jnp.exp(steps), dims[dim] // shards_of).reshape((-1,) + (1,) * (len(dims) - 1 - dim))
    return gain


def assign_block(stream_key, own, number, rows, amount, top, limit, lean):
    sequence = jax.random.permutation(stream_key, amount)
    crowded, common = load_shares(amount, rows * top, limit, lean, True), load_shares(amount, rows * top, limit, lean, False)
    places = jnp.arange(amount)

    def named(tallies, offset_by):
        used = int((tallies > 0).sum())
        fixed = max(1, used // 4)
        shifted = fixed + (places - fixed + offset_by * (used - fixed)) % max(1, amount - fixed)
        return jnp.zeros((amount,), jnp.int32).at[sequence[jnp.where(places < fixed, places, shifted)]].set(jnp.asarray(tallies, jnp.int32))

    tallies = jnp.where(number % 4 == 0, named(crowded, number // 4), named(common, number - number // 4 - 1))
    mixed = jax.random.permutation(jax.random.fold_in(own, 3), amount)
    giver, taker = mixed[0:amount // 2 * 2:2], mixed[1:amount // 2 * 2:2]
    margin = jnp.minimum(tallies[giver] - 1, limit - tallies[taker]) // 2
    margin = jnp.where((giver == sequence[0]) | (taker == sequence[0]) | (tallies[taker] == 0), 0, jnp.maximum(margin, 0))
    shifted = jax.random.randint(jax.random.fold_in(own, 4), (amount // 2,), 0, 1 << 20) % (margin + 1)
    tallies = tallies.at[giver].add(-shifted).at[taker].add(shifted)
    labels = jnp.searchsorted(jnp.cumsum(tallies), jnp.arange(rows * top), side="right").astype(jnp.int32)
    listing = labels.reshape(top, rows).T
    listing = listing[jax.random.permutation(jax.random.fold_in(own, 1), rows)]
    offset_by = jax.random.randint(jax.random.fold_in(own, 2), (rows, 1), 0, top)
    return jnp.take_along_axis(listing, (jnp.arange(top)[None, :] + offset_by) % top, axis=1)


def load_shares(number_of, total, reach, skew, full):
    portions = [(1 << 20) // math.isqrt(grade ** skew) + 1 for grade in range(1, number_of + 1)]
    largest = reach if full else min(reach, max(-(-total // number_of), total * portions[0] // sum(portions)))
    least = 1 if total - largest >= number_of - 1 else 0
    holding, rest = [largest] + [least] * (number_of - 1), total - largest - least * (number_of - 1)
    while rest > 0:
        movable = [i for i in range(1, number_of) if holding[i] < largest] or [i for i in range(1, number_of) if holding[i] < reach]
        whole, remaining = sum([portions[i] for i in movable]), rest
        for i in movable:
            more = min(reach - holding[i], max(1, remaining * portions[i] // whole), rest)
            holding[i] = holding[i] + more
            rest = rest - more
    return np.array(holding)


def normal_values(key, shape, deviation, bound, shards=(), held_as=jnp.bfloat16):
    drawn = deviation * jax.random.normal(key, shape, jnp.float32)
    if shards:
        drawn = drawn * levels(key, shape, shards, -0.22, 0.18)
    return jnp.clip(drawn, -bound, bound).astype(held_as)


def setup_inputs(seed: int = 0) -> dict:
    splits = jax.random.split(jax.random.key(seed), 11)
    tokens = normal_values(splits[0], (TOKENS, D), 1.0, 6.0, ((0, 8), (1, 4)))
    queries = draw_queries(jax.random.fold_in(splits[10], 71), 0)
    latents = draw_latents(jax.random.fold_in(splits[10], 71), 0)
    value_up = normal_values(splits[3], (HEADS, LAT, VDIM), LAT ** -0.5, 0.25, ((0, 4),))
    out_proj = normal_values(splits[4], (HEADS * VDIM, D), (HEADS * VDIM // 2) ** -0.5, 0.09375, ((0, 4), (1, 8)))
    expert_ids_keys = jax.random.split(jax.random.fold_in(splits[5], 1), TOKENS // TOK_DEV)
    expert_ids_turns = jax.random.permutation(jax.random.fold_in(splits[5], 3), TOKENS // TOK_DEV)
    expert_ids = jax.vmap(lambda own, number: assign_block(jax.random.fold_in(splits[5], 2), own, number, TOK_DEV, EXPERTS, TOPK, CAP, 2))(expert_ids_keys, expert_ids_turns).reshape((TOKENS, TOPK))
    expert_gates = jnp.clip(0.05 + 0.45 * jax.random.uniform(splits[6], (TOKENS, TOPK), jnp.float32) ** levels(splits[6], (TOKENS, TOPK), ((0, 8),), -0.2, 0.2), 0.05, 0.5)
    w_gate = normal_values(splits[7], (EXPERTS, D, FF), D ** -0.5, 0.09375, ((0, 8), (2, 4)))
    w_up = normal_values(splits[8], (EXPERTS, D, FF), D ** -0.5, 0.09375, ((0, 8), (2, 4)))
    w_down = normal_values(splits[9], (EXPERTS, FF, D), FF ** -0.5, 0.125, ((0, 8), (2, 4)))
    return {"tokens": tokens, "queries": queries, "latents": latents, "value_up": value_up, "out_proj": out_proj, "expert_ids": expert_ids, "expert_gates": expert_gates, "w_gate": w_gate, "w_up": w_up, "w_down": w_down}


def reference(tokens, queries, latents, value_up, out_proj, expert_ids, expert_gates, w_gate, w_up, w_down):
    score_scale = (QKNOPE + ROPE) ** (-0.5)
    key_width = LAT + ROPE
    positions = jnp.arange(TOKENS, dtype=jnp.int32)
    causal = positions[None, :] <= positions[:, None]
    values = latents[:, :LAT]
    query_heads = queries.reshape(TOKENS, HEADS, key_width).transpose(1, 0, 2)

    def one_head(inputs):
        query_one, lift_one = inputs
        scores = jnp.dot(query_one, latents.T, preferred_element_type=jnp.float32) * score_scale
        scores = jnp.where(causal, scores, -jnp.inf)
        row_max = lax.optimization_barrier(jnp.max(scores, axis=1, keepdims=True))
        weights = jnp.where(causal, jnp.exp(scores - row_max), 0.0)
        denominator = lax.optimization_barrier(jnp.sum(weights, axis=1, keepdims=True))
        context = (jnp.dot(weights.astype(jnp.bfloat16), values, preferred_element_type=jnp.float32) / denominator).astype(jnp.bfloat16)
        return jnp.dot(context, lift_one, preferred_element_type=jnp.float32).astype(jnp.bfloat16)
    lifted = lax.map(one_head, (query_heads, value_up))
    lifted = lifted.transpose(1, 0, 2).reshape(TOKENS, HEADS * VDIM)
    attended = jnp.dot(lifted, out_proj, preferred_element_type=jnp.float32)
    mid_state = (tokens.astype(jnp.float32) + attended).astype(jnp.bfloat16)
    mid_wide = mid_state.astype(jnp.float32)
    squares = lax.optimization_barrier(jnp.sum(mid_wide * mid_wide, axis=1))
    normed = (mid_wide * lax.rsqrt(squares / D + 1e-06)[:, None]).astype(jnp.bfloat16)
    most_load = N_BLK * CAP
    flat_ids = expert_ids.reshape(-1)
    flat_gates = expert_gates.reshape(-1)
    flat_tokens = jnp.arange(TOKENS * TOPK, dtype=jnp.int32) // TOPK

    def one_expert(expert):
        chosen = flat_ids == expert
        where_idx = jnp.nonzero(chosen, size=most_load, fill_value=0)[0].astype(jnp.int32)
        live = jnp.arange(most_load, dtype=jnp.int32) < jnp.sum(chosen.astype(jnp.int32))
        rows_in = normed[flat_tokens[where_idx]]
        gate_val = jnp.dot(rows_in, w_gate[expert], preferred_element_type=jnp.float32)
        up_val = jnp.dot(rows_in, w_up[expert], preferred_element_type=jnp.float32)
        activation = (jax.nn.silu(gate_val) * up_val).astype(jnp.bfloat16)
        expert_out = jnp.dot(activation, w_down[expert], preferred_element_type=jnp.float32).astype(jnp.bfloat16)
        weight_row = jnp.where(live, flat_gates[where_idx], 0.0)
        return (where_idx, expert_out.astype(jnp.float32) * weight_row[:, None])
    index_all, contrib = lax.map(one_expert, jnp.arange(EXPERTS, dtype=jnp.int32))
    routed = jnp.zeros((TOKENS * TOPK, D), jnp.float32).at[index_all.reshape(-1)].add(contrib.reshape(-1, D))
    routed = lax.optimization_barrier(jnp.sum(routed.reshape(TOKENS, TOPK, D), axis=1))
    return (mid_wide + routed).astype(jnp.bfloat16)
```

```python
import functools

import jax
import jax.numpy as jnp
from jax import lax
from jax.experimental import pallas as pl
from jax.experimental.pallas import tpu as pltpu
from jax.sharding import PartitionSpec as P

D = 4096
LAT = 512
ROPE = 64
QKNOPE = 128
EXPERTS = 32
CAP = 20


def lifted_heads(queries, latents, value_up):
    row_count = latents.shape[0]
    heads_here = value_up.shape[0]
    first_row = lax.axis_index("blk") * row_count
    score_scale = (QKNOPE + ROPE) ** (-0.5)
    query_heads = queries.reshape(row_count, heads_here, LAT + ROPE)
    query_pos = first_row + jnp.arange(row_count, dtype=jnp.int32)
    last_query = first_row + row_count - 1
    start_state = (
        jnp.full((row_count, heads_here), -1e30, jnp.float32),
        jnp.zeros((row_count, heads_here), jnp.float32),
        jnp.zeros((row_count, heads_here, LAT), jnp.float32),
    )
    segment = lax.all_gather(latents, "blk", axis=0, tiled=True)

    def compute(state_in):
        running_max, denominator, accumulated = state_in
        key_count = segment.shape[0]
        scores = (
            jnp.einsum("qhc,kc->qhk", query_heads, segment, preferred_element_type=jnp.float32)
            * score_scale
        )
        key_pos = jnp.arange(key_count, dtype=jnp.int32)
        allowed = (key_pos[None, :] <= query_pos[:, None])[:, None, :]
        scores = jnp.where(allowed, scores, -1e30)
        new_max = jnp.maximum(running_max, jnp.max(scores, axis=2))
        exp_weights = jnp.where(allowed, jnp.exp(scores - new_max[:, :, None]), 0.0)
        denominator = jnp.sum(exp_weights, axis=2)
        accumulated = jnp.einsum(
            "qhk,kc->qhc",
            exp_weights.astype(jnp.bfloat16),
            segment[:, :LAT],
            preferred_element_type=jnp.float32,
        )
        return (new_max, denominator, accumulated)

    def keep(state_in):
        return state_in

    running_max, denominator, accumulated = lax.cond(
        jnp.int32(0) <= last_query, compute, keep, start_state
    )
    context = (accumulated / denominator[:, :, None]).astype(jnp.bfloat16)
    lifted = jnp.einsum(
        "qhc,hcv->qhv", context, value_up, preferred_element_type=jnp.float32
    ).astype(jnp.bfloat16)
    lifted = lifted.reshape(row_count, heads_here * value_up.shape[2])
    return lifted


def by_collectives(
    tokens, queries, latents, value_up, out_proj, expert_ids, expert_gates, w_gate, w_up, w_down
):
    row_count = tokens.shape[0]
    lifted = lifted_heads(queries, latents, value_up)
    spread_out = jnp.dot(
        lax.all_gather(lifted, "blk", axis=0, tiled=True),
        out_proj,
        preferred_element_type=jnp.float32,
    )
    partial_out = lax.all_to_all(
        spread_out.astype(jnp.bfloat16), "blk", split_axis=0, concat_axis=1, tiled=True
    ).astype(spread_out.dtype)
    attended = lax.psum_scatter(
        partial_out.astype(jnp.bfloat16), "head", scatter_dimension=1, tiled=True
    ).astype(jnp.float32)
    mid_state = (tokens.astype(jnp.float32) + attended).astype(jnp.bfloat16)
    mid_wide = mid_state.astype(jnp.float32)
    squares = lax.psum(jnp.sum(mid_wide * mid_wide, axis=1), "head")
    normed = (mid_wide * lax.rsqrt(squares / D + 1e-06)[:, None]).astype(jnp.bfloat16)
    flat_ids = expert_ids.reshape(-1)
    choose_count = expert_ids.shape[1]
    onehot_ids = (flat_ids[:, None] == jnp.arange(EXPERTS, dtype=jnp.int32)[None, :]).astype(
        jnp.int32
    )
    earlier = jnp.cumsum(onehot_ids, axis=0) - onehot_ids
    ranks = jnp.sum(earlier * onehot_ids, axis=1)
    slot_ids = flat_ids * CAP + ranks
    slot_hits = jnp.arange(EXPERTS * CAP, dtype=jnp.int32)[:, None] == slot_ids[None, :]
    select = jnp.sum(
        slot_hits.astype(jnp.bfloat16).reshape(EXPERTS * CAP, row_count, choose_count), axis=2
    )
    combine = jnp.sum(
        jnp.where(slot_hits, expert_gates.reshape(-1)[None, :], 0.0).reshape(
            EXPERTS * CAP, row_count, choose_count
        ),
        axis=2,
    )
    outgoing = (
        jnp.dot(select, normed, preferred_element_type=jnp.float32)
        .astype(jnp.bfloat16)
        .reshape(EXPERTS, CAP, normed.shape[1])
    )
    incoming = lax.all_to_all(outgoing, "blk", split_axis=0, concat_axis=1, tiled=True)
    contract_segment = lax.all_gather(incoming, "head", axis=2, tiled=True)
    gate_add = jnp.einsum(
        "esd,edf->esf", contract_segment, w_gate, preferred_element_type=jnp.float32
    )
    up_add = jnp.einsum("esd,edf->esf", contract_segment, w_up, preferred_element_type=jnp.float32)
    activation = (jax.nn.silu(gate_add) * up_add).astype(jnp.bfloat16)
    expert_out = jnp.einsum(
        "esf,efd->esd",
        lax.all_gather(activation, "head", axis=2, tiled=True),
        w_down,
        preferred_element_type=jnp.float32,
    ).astype(jnp.bfloat16)
    returned = lax.all_to_all(expert_out, "blk", split_axis=1, concat_axis=0, tiled=True)
    returned_wide = returned.reshape(EXPERTS * CAP, returned.shape[2]).astype(jnp.float32)
    routed = jnp.einsum("sr,sd->rd", combine, returned_wide, precision=lax.Precision.HIGHEST)
    return (mid_wide + routed).astype(jnp.bfloat16)


MESH = pl.DeviceIdType.MESH


def push(src, dst, send, recv, device):
    return pltpu.make_async_remote_copy(
        src_ref=src, dst_ref=dst, send_sem=send, recv_sem=recv, device_id=device, device_id_type=MESH
    )


def greet(peers):
    barrier = pltpu.get_barrier_semaphore()
    for peer in peers:
        pl.semaphore_signal(barrier, inc=1, device_id=peer, device_id_type=MESH)
    pl.semaphore_wait(barrier, len(peers))


def mid_kernel(
    nb, nh, lifted_ref, piece_ref, proj_ref, mid_ref, gathered, partial, arrived, own,
    lift_send, lift_recv, side_send, side_recv, sum_send, sum_recv,
    z_send, z_recv, g_send, g_recv, c_send, c_recv,
):
    b, h = lax.axis_index("blk"), lax.axis_index("head")
    groups = nb // 2
    g, c = b // 2, b % 2
    rows = lifted_ref.shape[0]
    tall, wide = piece_ref.shape
    sibling = (g * 2 + 1 - c, h)

    def to_g(k):
        return (g + k) % groups

    def from_g(k):
        return (g + groups - k) % groups

    def to_h(k):
        return (h + k) % nh

    def from_h(k):
        return (h + nh - k) % nh

    greet(
        [sibling]
        + [(to_g(k) * 2 + c, h) for k in range(1, groups)]
        + [(b, to_h(k)) for k in range(1, nh)]
    )

    def block(owner):
        return gathered.at[pl.ds(pl.multiple_of(owner * rows, rows), rows), :]

    sends = []

    def launch(copy):
        copy.start()
        sends.append(copy)

    for k in range(1, groups):
        launch(
            push(lifted_ref, block(b), lift_send.at[k], lift_recv.at[k], (to_g(k) * 2 + c, h))
        )
    launch(push(lifted_ref, block(b), side_send.at[0], side_recv.at[0], sibling))
    gathered[pl.ds(pl.multiple_of(b * rows, rows), rows), :] = lifted_ref[...]

    def attend(k):
        group = from_g(k)
        theirs = block(group * 2 + 1 - c)
        push(theirs, theirs, side_send.at[k], side_recv.at[k], sibling).wait_recv()
        both = gathered[pl.ds(pl.multiple_of(group * tall, tall), tall), :]
        out = jnp.dot(both, proj_ref[...], preferred_element_type=jnp.float32)

        @pl.when(group == h)
        def _():
            own[...] = out

        @pl.when(group != h)
        def _():
            partial[group] = out.astype(jnp.bfloat16)
            push(
                partial.at[group], arrived.at[h], sum_send.at[group], sum_recv.at[h], (b, group)
            ).start()

    for k in range(1, groups):
        mine = block(from_g(k) * 2 + c)
        push(mine, mine, lift_send.at[k], lift_recv.at[k], sibling).wait_recv()
        launch(push(mine, mine, side_send.at[k], side_recv.at[k], sibling))
        attend(k - 1)
    attend(groups - 1)

    total = own[...] + piece_ref[...].astype(jnp.float32)
    for k in range(1, nh):
        theirs = arrived.at[from_h(k)]
        push(theirs, theirs, sum_send.at[0], sum_recv.at[from_h(k)], sibling).wait_recv()
        total = total + arrived[from_h(k)].astype(jnp.float32)

    def place(head, owner):
        return mid_ref.at[
            pl.ds(pl.multiple_of(head * tall, tall), tall),
            pl.ds(pl.multiple_of(owner * wide, wide), wide),
        ]

    mid_ref[
        pl.ds(pl.multiple_of(h * tall, tall), tall), pl.ds(pl.multiple_of(b * wide, wide), wide)
    ] = total.astype(jnp.bfloat16)

    at = place(h, b)
    for k in range(1, nh):
        launch(push(at, at, z_send.at[k], z_recv.at[k], (b, to_h(k))))
    for kz in range(nh):
        at = place(from_h(kz), b)
        if kz > 0:
            push(at, at, z_send.at[kz], z_recv.at[kz], sibling).wait_recv()
        for k in range(1, groups):
            launch(push(at, at, g_send.at[kz, k], g_recv.at[kz, k], (to_g(k) * 2 + c, h)))
        launch(push(at, at, c_send.at[kz, 0], c_recv.at[kz, 0], sibling))
    for kz in range(nh):
        for k in range(1, groups):
            at = place(from_h(kz), from_g(k) * 2 + c)
            push(at, at, g_send.at[kz, k], g_recv.at[kz, k], sibling).wait_recv()
            launch(push(at, at, c_send.at[kz, k], c_recv.at[kz, k], sibling))
    for kz in range(nh):
        for k in range(groups):
            at = place(from_h(kz), from_g(k) * 2 + 1 - c)
            push(at, at, c_send.at[kz, k], c_recv.at[kz, k], sibling).wait_recv()
    for copy in sends:
        copy.wait_send()
    for k in range(1, nh):
        out = partial.at[to_h(k)]
        push(out, out, sum_send.at[to_h(k)], sum_recv.at[0], sibling).wait_send()


def mid_states(nb, nh, lifted, piece, out_proj):
    rows, depth = lifted.shape
    tall, wide = piece.shape
    groups = nb // 2
    dma = pltpu.SemaphoreType.DMA
    vmem = pl.BlockSpec(memory_space=pltpu.VMEM)
    return pl.pallas_call(
        functools.partial(mid_kernel, nb, nh),
        out_shape=jax.ShapeDtypeStruct((rows * nb, wide * nb), jnp.bfloat16),
        in_specs=[vmem] * 3,
        out_specs=vmem,
        scratch_shapes=[
            pltpu.VMEM((nb * rows, depth), jnp.bfloat16),
            pltpu.VMEM((nh, tall, wide), jnp.bfloat16),
            pltpu.VMEM((nh, tall, wide), jnp.bfloat16),
            pltpu.VMEM((tall, wide), jnp.float32),
            dma((groups,)), dma((groups,)), dma((groups,)), dma((groups,)),
            dma((nh,)), dma((nh,)), dma((nh,)), dma((nh,)),
            dma((nh, groups)), dma((nh, groups)), dma((nh, groups)), dma((nh, groups)),
        ],
        compiler_params=pltpu.CompilerParams(
            collective_id=0, has_side_effects=True, vmem_limit_bytes=40 * 2**20
        ),
        cost_estimate=pl.CostEstimate(
            flops=2 * nb * rows * depth * wide, bytes_accessed=2**23, transcendentals=0
        ),
        name="mid_states",
    )(lifted, piece, out_proj)


def expert_kernel(
    nb, nh, mid_ref, select_ref, spread_ref, gate_ref, wg_hbm, wu_hbm, wd_hbm, out_ref,
    wg, wu, wd, normed, picked, acts, acc, leaving, coming,
    wg_sem, wu_sem, wd_sem, up_send, down_send, act_recv, back_send, back_recv,
):
    b, h = lax.axis_index("blk"), lax.axis_index("head")
    experts, slots, count = select_ref.shape
    hidden = wg.shape[2]
    rows, cols = out_ref.shape
    width = mid_ref.shape[1]

    def first(e):
        return [
            pltpu.make_async_copy(wg_hbm.at[e], wg.at[e % 2], wg_sem.at[e % 2]),
            pltpu.make_async_copy(wu_hbm.at[e], wu.at[e % 2], wu_sem.at[e % 2]),
        ]

    def second(e):
        return pltpu.make_async_copy(wd_hbm.at[e], wd.at[e % 2], wd_sem.at[e % 2])

    for e in range(min(2, experts)):
        for copy in first(e):
            copy.start()
    for e in range(min(2, experts)):
        second(e).start()

    barrier = pltpu.get_barrier_semaphore()
    for k in range(1, nb):
        pl.semaphore_signal(barrier, inc=1, device_id=((b + k) % nb, h), device_id_type=MESH)
    for k in range(1, nh):
        pl.semaphore_signal(barrier, inc=1, device_id=(b, (h + k) % nh), device_id_type=MESH)

    chunk = 32

    @pl.loop(0, count // chunk)
    def _(i):
        at = pl.ds(pl.multiple_of(i * chunk, chunk), chunk)
        some = mid_ref[at, :].astype(jnp.float32)
        mean = jnp.sum(some * some, axis=1, keepdims=True) / width
        normed[at, :] = (some * lax.rsqrt(mean + 1e-06)).astype(jnp.bfloat16)

    acc[...] = jnp.zeros_like(acc)
    pl.semaphore_wait(barrier, nb + nh - 2)

    def shard(e, s):
        return acts.at[e, s]

    def up(e, s):
        return push(shard(e, s), shard(e, s), up_send.at[e, s], act_recv.at[e, s], (b, h + 1))

    def down(e, s):
        return push(shard(e, s), shard(e, s), down_send.at[e, s], act_recv.at[e, s], (b, h - 1))

    def came(e, s):
        push(shard(e, s), shard(e, s), up_send.at[e, s], act_recv.at[e, s], ((b + 1) % nb, h)).wait_recv()

    def onward(e, d):
        @pl.when(h - d >= 0)
        def _():
            if d > 0:
                came(e, h - d)

            @pl.when(h + 1 < nh)
            def _():
                up(e, h - d).start()

        @pl.when(h + d < nh)
        def _():
            if d > 0:
                came(e, h + d)

            @pl.when(h - 1 >= 0)
            def _():
                down(e, h + d).start()

    def raise_up(e):
        for copy in first(e):
            copy.wait()
        tile = 512

        @pl.loop(0, width // tile)
        def _(j):
            at = pl.ds(pl.multiple_of(j * tile, tile), tile)
            picked[:, at] = jnp.dot(
                select_ref[e], normed[:, at], preferred_element_type=jnp.float32
            ).astype(jnp.bfloat16)

        rows_in = picked[...]
        gate = jnp.dot(rows_in, wg[e % 2], preferred_element_type=jnp.float32)
        more = jnp.dot(rows_in, wu[e % 2], preferred_element_type=jnp.float32)
        acts[e, h] = (gate / (1.0 + jnp.exp(-gate)) * more).astype(jnp.bfloat16)
        if e + 2 < experts:
            for copy in first(e + 2):
                copy.start()

    def bring_down(e):
        second(e).wait()
        out = jnp.dot(acts[e, 0], wd[e % 2, 0:hidden], preferred_element_type=jnp.float32)
        for s in range(1, nh):
            out = out + jnp.dot(
                acts[e, s], wd[e % 2, s * hidden : (s + 1) * hidden],
                preferred_element_type=jnp.float32,
            )
        picked[:, 0:cols] = out.astype(jnp.bfloat16)
        if e + 2 < experts:
            second(e + 2).start()

        tile = 256
        for j in range(cols // tile):
            at = slice(j * tile, (j + 1) * tile)
            acc[:, at] += gate_ref[:, e : e + 1] * jnp.dot(
                spread_ref[e], picked[:, at], preferred_element_type=jnp.float32
            )

    for t in range(experts + nh - 1):
        if t < experts:
            raise_up(t)
            onward(t, 0)
        for d in range(1, nh):
            if 0 <= t - d < experts:
                onward(t - d, d)
        if 0 <= t - nh + 1 < experts:
            bring_down(t - nh + 1)

    backs = []
    for k in range(1, nb):
        to = (b + k) % nb
        leaving[k] = acc[pl.ds(pl.multiple_of(to * rows, rows), rows), :].astype(jnp.bfloat16)
        copy = push(leaving.at[k], coming.at[k], back_send.at[k], back_recv.at[k], (to, h))
        copy.start()
        backs.append(copy)
    mine = pl.ds(pl.multiple_of(b * rows, rows), rows)
    total = mid_ref[mine, pl.ds(pl.multiple_of(h * cols, cols), cols)].astype(jnp.float32)
    total = total + acc[mine, :]
    for k in range(1, nb):
        backs[k - 1].wait_recv()
        total = total + coming[k].astype(jnp.float32)
    out_ref[...] = total.astype(jnp.bfloat16)
    for copy in backs:
        copy.wait_send()
    for e in range(experts):
        for s in range(nh):

            @pl.when((h >= s) & (h + 1 < nh))
            def _(e=e, s=s):
                up(e, s).wait_send()

            @pl.when((h <= s) & (h - 1 >= 0))
            def _(e=e, s=s):
                down(e, s).wait_send()


def expert_layer(nb, nh, mid, select, spread, gates, w_gate, w_up, w_down):
    experts, width, hidden = w_gate.shape
    full, cols = w_down.shape[1:]
    slots, count = select.shape[1:]
    rows = count // nb
    dma = pltpu.SemaphoreType.DMA
    vmem = pl.BlockSpec(memory_space=pltpu.VMEM)
    hbm = pl.BlockSpec(memory_space=pl.ANY)
    return pl.pallas_call(
        functools.partial(expert_kernel, nb, nh),
        out_shape=jax.ShapeDtypeStruct((rows, cols), jnp.bfloat16),
        in_specs=[vmem] * 4 + [hbm] * 3,
        out_specs=vmem,
        scratch_shapes=[
            pltpu.VMEM((2, width, hidden), jnp.bfloat16),
            pltpu.VMEM((2, width, hidden), jnp.bfloat16),
            pltpu.VMEM((2, full, cols), jnp.bfloat16),
            pltpu.VMEM((count, width), jnp.bfloat16),
            pltpu.VMEM((slots, width), jnp.bfloat16),
            pltpu.VMEM((experts, nh, slots, hidden), jnp.bfloat16),
            pltpu.VMEM((count, cols), jnp.float32),
            pltpu.VMEM((nb, rows, cols), jnp.bfloat16),
            pltpu.VMEM((nb, rows, cols), jnp.bfloat16),
            dma((2,)), dma((2,)), dma((2,)),
            dma((experts, nh)), dma((experts, nh)), dma((experts, nh)),
            dma((nb,)), dma((nb,)),
        ],
        compiler_params=pltpu.CompilerParams(
            collective_id=1, has_side_effects=True, vmem_limit_bytes=58 * 2**20
        ),
        cost_estimate=pl.CostEstimate(
            flops=6 * experts * slots * width * hidden,
            bytes_accessed=6 * experts * width * hidden,
            transcendentals=0,
        ),
        name="expert_layer",
    )(mid, select, spread, gates, w_gate, w_up, w_down)


def by_kernels(
    nb, nh,
    tokens, queries, latents, value_up, out_proj, expert_ids, expert_gates, w_gate, w_up, w_down,
):
    b = lax.axis_index("blk")
    rows, cols = tokens.shape
    ratio = nb // nh
    part = cols // ratio
    top = expert_ids.shape[1]
    here = w_gate.shape[0]
    slots = CAP * nb

    routes = lax.all_gather(
        jnp.concatenate([expert_ids.astype(jnp.float32), expert_gates], axis=1),
        "blk", axis=0, tiled=True,
    )
    piece = jnp.zeros((rows * ratio, part), tokens.dtype)
    for p in range(ratio):
        turn = (p + b) % ratio
        moved = lax.ppermute(
            lax.dynamic_slice(tokens, (0, turn * part), (rows, part)),
            ("blk", "head"),
            [
                (i * nh + j, (ratio * j + (p + i) % ratio) * nh + i // ratio)
                for i in range(nb)
                for j in range(nh)
            ],
        )
        piece = lax.dynamic_update_slice(piece, moved, ((b + ratio - p) % ratio * rows, 0))

    ids = routes[:, :top].astype(jnp.int32)
    hits = ids[:, :, None] == (b * here + jnp.arange(here, dtype=jnp.int32))[None, None, :]
    member = jnp.any(hits, axis=1)
    gates = jnp.sum(jnp.where(hits, routes[:, top:, None], 0.0), axis=1)
    order = jnp.arange(member.shape[0], dtype=jnp.int32)
    rank = jnp.dot(
        (order[:, None] > order[None, :]).astype(jnp.bfloat16),
        member.astype(jnp.bfloat16),
        preferred_element_type=jnp.float32,
    ).astype(jnp.int32)
    slot = jnp.where(member, rank, -1)
    lanes = jnp.arange(slots, dtype=jnp.int32)
    select = (slot.T[:, None, :] == lanes[None, :, None]).astype(jnp.bfloat16)
    spread = (slot.T[:, :, None] == lanes[None, None, :]).astype(jnp.bfloat16)

    lifted = lifted_heads(queries, latents, value_up)
    mid = mid_states(nb, nh, lifted, piece, out_proj)
    return expert_layer(nb, nh, mid, select, spread, gates, w_gate, w_up, w_down)


def fitting(mesh):
    nb, nh = mesh.shape["blk"], mesh.shape["head"]
    if nb == 2 * nh and nb * nh <= 32:
        return functools.partial(by_kernels, nb, nh)
    return by_collectives


def solution(mesh):
    placed = (
        P("blk", "head"),
        P("blk", "head"),
        P("blk", None),
        P("head", None, None),
        P("head", "blk"),
        P("blk", None),
        P("blk", None),
        P("blk", None, "head"),
        P("blk", None, "head"),
        P("blk", None, "head"),
    )
    return jax.shard_map(
        fitting(mesh), mesh=mesh, in_specs=placed, out_specs=P("blk", "head"), check_vma=False
    )
```
